1024 devices in a mesh: grp: 16 (over x, y), dev: 64 (over z, core).
Axes of the slice: x: 4, y: 4, z: 32, core: 2. Of those that a mesh axis runs over, the one named last changes fastest.
Arguments:
- papers: bfloat16 [262144, 768], P(('grp', 'dev')), may hold values from -6 to 6
- authors: bfloat16 [262144, 768], P(('grp', 'dev')), may hold values from -6 to 6
- cotangent: bfloat16 [262144, 512], P(('grp', 'dev')), may hold values from -6 to 6
- w_self: bfloat16 [768, 512], replicated, may hold values from -0.21875 to 0.21875
- w_cite: bfloat16 [768, 512], replicated, may hold values from -0.21875 to 0.21875
- w_aut: bfloat16 [768, 512], replicated, may hold values from -0.21875 to 0.21875
- bias: float32 [512], replicated, may hold values from -3 to 3
- cite_col: int32 [262144, 8], P(('grp', 'dev')), may hold values from 0 to 383
- edge_author: int32 [262144], P(('grp', 'dev')), may hold values from 0 to 255
- edge_dest: int32 [262144, 1], P(('grp', 'dev')), may hold values from 0 to 63; in each aligned block of 256 rows (0 to 255, 256 to 511, ...) at most 8 rows name the same one
- edge_row: int32 [262144], P(('grp', 'dev')), may hold values from 0 to 255
Outputs:
- updated: bfloat16 [262144, 512], P(('grp', 'dev'))
- grad_authors: bfloat16 [262144, 768], P(('grp', 'dev'))
- grad_w_aut: float32 [768, 512], replicated
The draws below stay inside these ranges and needn't reach their ends.
Inputs may be any that keep to these rules, and one draw needn't show every extreme that they name: `edge_dest`: among the 256 edges of one device no destination appears more than 8 times, and some destination appears exactly 8 times.
All inputs are finite; a program needn't handle non-finite values.
Results may differ from the reference program's by a relative error of at most 0.0056.
Values may be sent and summed in bfloat16 or wider, within the bound.
No kernel may reach another device: no remote copies, remote signals or barrier semaphores. Data moves between devices by JAX's collectives and lax.ppermute only.
A program may use at most 32 MiB of HBM per device.

```python
import math
import jax
import jax.numpy as jnp
import numpy as np
from jax import lax

D = 768
H = 512
PAP_DEV = 256
AUT_DEV = 256
EDGE_DEV = 256
RIM = 64
K_CIT = 8
CAP = 8
PAPERS = 262144
AUTHORS = 262144
EDGES = 262144
N_GRP = 16
N_DEV = 64


def set_ends(result, key, low, high):
    longest = result.shape.index(max(result.shape))
    spots = []
    for shift in (0, 1):
        where = [jax.random.randint(jax.random.fold_in(key, axis), (), 0, length) for axis, length in enumerate(result.shape)]
        where[longest] = (where[longest] + shift) % result.shape[longest]
        spots.append(tuple(where))
    return result.at[spots[0]].set(low).at[spots[1]].set(high)


def block_levels(key, shape, pieces, smallest, high):
    def one(axis_at, blocks):
        draws = jax.random.uniform(jax.random.fold_in(jax.random.fold_in(key, 6), axis_at), (blocks,), jnp.float32, smallest / len(pieces), high / len(pieces))
        return jnp.repeat(jnp.exp(draws), shape[axis_at] // blocks).reshape((-1,) + (1,) * (len(shape) - axis_at - 1))

    factor_of = one(*pieces[0])
    for cut in pieces[1:]:
        factor_of = factor_of * one(*cut)
    return factor_of


def routed_block(own_key, own, number, rows, number_of, top, limit, skew):
    ranking = jax.random.permutation(own_key, number_of)
    packed, ordinary = load_shares(number_of, rows * top, limit, skew, True), load_shares(number_of, rows * top, limit, skew, False)
    places = jnp.arange(number_of)

    def named(sizes, turn):
        used = int((sizes > 0).sum())
        fixed = max(1, used // 4)
        moved = fixed + (places - fixed + turn * (used - fixed)) % max(1, number_of - fixed)
        return jnp.zeros((number_of,), jnp.int32).at[ranking[jnp.where(places < fixed, places, moved)]].set(jnp.asarray(sizes, jnp.int32))

    sizes = jnp.where(number % 4 == 0, named(packed, number // 4), named(ordinary, number - number // 4 - 1))
    mixed = jax.random.permutation(jax.random.fold_in(own, 3), number_of)
    giver, receiver = mixed[0:number_of // 2 * 2:2], mixed[1:number_of // 2 * 2:2]
    room = jnp.minimum(sizes[giver] - 1, limit - sizes[receiver]) // 2
    room = jnp.where((giver == ranking[0]) | (receiver == ranking[0]) | (sizes[receiver] == 0), 0, jnp.maximum(room, 0))
    moved = jax.random.randint(jax.random.fold_in(own, 4), (number_of // 2,), 0, 1 << 20) % (room + 1)
    sizes = sizes.at[giver].add(-moved).at[receiver].add(moved)
    items = jnp.searchsorted(jnp.cumsum(sizes), jnp.arange(rows * top), side="right").astype(jnp.int32)
    table = items.reshape(top, rows).T
    table = table[jax.random.permutation(jax.random.fold_in(own, 1), rows)]
    turn = jax.random.randint(jax.random.fold_in(own, 2), (rows, 1), 0, top)
    return jnp.take_along_axis(table, (jnp.arange(top)[None, :] + turn) % top, axis=1)


def load_shares(number_of, total, limit, slope, full):
    loads = [(1 << 20) // math.isqrt(standing ** slope) + 1 for standing in range(1, number_of + 1)]
    largest = limit if full else min(limit, max(-(-total // number_of), total * loads[0] // sum(loads)))
    least = 1 if total - largest >= number_of - 1 else 0
    holding, spare = [largest] + [least] * (number_of - 1), total - largest - least * (number_of - 1)
    while spare > 0:
        candidates = [i for i in range(1, number_of) if holding[i] < largest] or [i for i in range(1, number_of) if holding[i] < limit]
        pool, left = sum([loads[i] for i in candidates]), spare
        for i in candidates:
            extra = min(limit - holding[i], max(1, left * loads[i] // pool), spare)
            holding[i] = holding[i] + extra
            spare = spare - extra
    return np.array(holding)


def bell_draw(stream_key, shape, spread, most, cuts=(), kind=jnp.bfloat16):
    values = jax.random.normal(stream_key, shape, jnp.float32) * spread
    if len(cuts) > 0:
        values = block_levels(stream_key, shape, cuts, -0.22, 0.18) * values
    return jnp.clip(values, min=-most, max=most).astype(kind)


def setup_inputs(seed: int = 0) -> dict:
    key_of = jax.random.split(jax.random.key(seed), 12)
    papers = bell_draw(key_of[0], (PAPERS, D), 1.0, 6.0, ((0, 1024),))
    authors = bell_draw(key_of[1], (AUTHORS, D), 1.0, 6.0, ((0, 1024),))
    cotangent = bell_draw(key_of[2], (PAPERS, H), 1.0, 6.0, ((0, 1024),))
    w_self = bell_draw(key_of[3], (D, H), D ** -0.5, 0.21875)
    w_cite = bell_draw(key_of[4], (D, H), D ** -0.5, 0.21875)
    w_aut = bell_draw(key_of[5], (D, H), D ** -0.5, 0.21875)
    bias = bell_draw(key_of[6], (H,), 0.5, 3.0, (), jnp.float32)
    cite_col = set_ends(jax.random.randint(key_of[7], (PAPERS, K_CIT), 0, PAP_DEV + 2 * RIM), jax.random.fold_in(key_of[7], 1), 0, (PAP_DEV + 2 * RIM) - 1).astype(jnp.int32)
    edge_author = set_ends(jax.random.randint(key_of[8], (EDGES,), 0, AUT_DEV), jax.random.fold_in(key_of[8], 1), 0, AUT_DEV - 1).astype(jnp.int32)
    edge_dest_keys = jax.random.split(jax.random.fold_in(key_of[9], 1), EDGES // EDGE_DEV)
    edge_dest_turns = jax.random.permutation(jax.random.fold_in(key_of[9], 3), EDGES // EDGE_DEV)
    edge_dest = jax.vmap(lambda own, number: routed_block(jax.random.fold_in(key_of[9], 2), own, number, EDGE_DEV, N_DEV, 1, CAP, 2))(edge_dest_keys, edge_dest_turns).reshape((EDGES, 1))
    edge_row = set_ends(jax.random.randint(key_of[10], (EDGES,), 0, PAP_DEV), jax.random.fold_in(key_of[10], 1), 0, PAP_DEV - 1).astype(jnp.int32)
    return {"papers": papers, "authors": authors, "cotangent": cotangent, "w_self": w_self, "w_cite": w_cite, "w_aut": w_aut, "bias": bias, "cite_col": cite_col, "edge_author": edge_author, "edge_dest": edge_dest, "edge_row": edge_row}


def reference(papers, authors, cotangent, w_self, w_cite, w_aut, bias, cite_col, edge_author, edge_dest, edge_row):
    blocks = N_GRP * N_DEV
    grouped = papers.reshape(N_GRP, N_DEV, PAP_DEV, D)
    zeros_rim = jnp.zeros((N_GRP, 1, RIM, D), papers.dtype)
    before = jnp.concatenate([zeros_rim, grouped[:, :-1, PAP_DEV - RIM:]], axis=1).reshape(blocks, RIM, D)
    after = jnp.concatenate([grouped[:, 1:, :RIM], zeros_rim], axis=1).reshape(blocks, RIM, D)
    own_rows = papers.reshape(blocks, PAP_DEV, D)
    columns = cite_col.reshape(blocks, PAP_DEV, K_CIT)

    def cite_block(index):
        extended = jnp.concatenate([before[index], own_rows[index], after[index]], axis=0)
        picked = jnp.take(extended, columns[index], axis=0).astype(jnp.float32)
        return (lax.optimization_barrier(jnp.sum(picked, axis=1)) / K_CIT).astype(jnp.bfloat16)
    cite_agg = lax.map(cite_block, jnp.arange(blocks, dtype=jnp.int32)).reshape(PAPERS, D)
    proj = jnp.dot(authors, w_aut, preferred_element_type=jnp.float32).astype(jnp.bfloat16)
    edge_ids = jnp.arange(EDGES, dtype=jnp.int32)
    source = edge_ids // EDGE_DEV * AUT_DEV + edge_author
    group_of = edge_ids // (N_DEV * EDGE_DEV)
    target = (group_of * N_DEV + edge_dest[:, 0]) * PAP_DEV + edge_row
    messages = jnp.take(proj, source, axis=0).astype(jnp.float32)
    aut_sum = jax.ops.segment_sum(messages, target, num_segments=PAPERS)
    count = jax.ops.segment_sum(jnp.ones((EDGES,), jnp.float32), target, num_segments=PAPERS)
    inverse = 1.0 / jnp.maximum(count, 1.0)
    pre = jnp.dot(papers, w_self, preferred_element_type=jnp.float32)
    pre = pre + jnp.dot(cite_agg, w_cite, preferred_element_type=jnp.float32)
    pre = pre + aut_sum * inverse[:, None] + bias[None, :]
    sigma = jax.nn.sigmoid(pre)
    updated = (pre * sigma).astype(jnp.bfloat16)
    delta = cotangent.astype(jnp.float32) * sigma * (1.0 + pre * (1.0 - sigma))
    scaled = delta * inverse[:, None]
    edge_grad = jnp.take(scaled, target, axis=0).astype(jnp.bfloat16)
    grad_proj = jax.ops.segment_sum(edge_grad.astype(jnp.float32), source, num_segments=AUTHORS).astype(jnp.bfloat16)
    grad_authors = jnp.dot(grad_proj, w_aut.T, preferred_element_type=jnp.float32).astype(jnp.bfloat16)
    grad_w_aut = jnp.dot(authors.T, grad_proj, preferred_element_type=jnp.float32) / jnp.sqrt(jnp.float32(AUTHORS))
    return (updated, grad_authors, grad_w_aut)
```

```python
import functools
import math

import jax
import jax.numpy as jnp
from jax import lax
from jax.experimental import pallas as pl
from jax.experimental.pallas import tpu as pltpu
from jax.sharding import PartitionSpec as P

RIM = 64
K_CIT = 8
AUX = 128
BF = jnp.bfloat16
F32 = jnp.float32
NN = (((1,), (0,)), ((), ()))
NT = (((1,), (1,)), ((), ()))
TN = (((0,), (0,)), ((), ()))


def mm(a, b, dims):
    return lax.dot_general(a, b, dims, preferred_element_type=F32)


def call(kernel, outs, args, flops):
    moved = sum(math.prod(a.shape) * a.dtype.itemsize for a in list(args) + list(outs))
    return pl.pallas_call(
        kernel,
        out_shape=outs,
        compiler_params=pltpu.CompilerParams(vmem_limit_bytes=24 * 1024 * 1024),
        cost_estimate=pl.CostEstimate(flops=flops, bytes_accessed=moved, transcendentals=0),
    )(*args)


def pack_kernel(devs, authors, author, dest, row, out, owner):
    edges = author.shape[1]
    auts = authors.shape[0]
    width = authors.shape[1]
    total = out.shape[0]
    cap = total // devs
    dest_of = dest[...]
    hot = (lax.broadcasted_iota(jnp.int32, (devs, edges), 0) == dest_of).astype(F32)
    before = (
        lax.broadcasted_iota(jnp.int32, (edges, edges), 0)
        < lax.broadcasted_iota(jnp.int32, (edges, edges), 1)
    ).astype(F32)
    earlier = mm(hot.astype(BF), before.astype(BF), NN)
    rank = jnp.sum(hot * earlier, axis=0, keepdims=True)
    position = dest_of * cap + rank.astype(jnp.int32)
    slot_edge = (
        (lax.broadcasted_iota(jnp.int32, (total, edges), 0) == position).astype(F32).astype(BF)
    )
    author_edge = (
        (lax.broadcasted_iota(jnp.int32, (auts, edges), 0) == author[...]).astype(F32).astype(BF)
    )
    slot_author = mm(slot_edge, author_edge, NT).astype(BF)
    owner[...] = slot_author
    out[:, :width] = mm(slot_author, authors[...], NN).astype(BF)
    lane = lax.broadcasted_iota(jnp.int32, (AUX, edges), 0)
    aux = jnp.where(lane == 0, row[...] + 1, jnp.where(lane == 1, 1, 0)).astype(F32).astype(BF)
    out[:, width:] = mm(slot_edge, aux, NT).astype(BF)


def base_kernel(papers, low, high, cite, w_self, w_cite, bias, base):
    rows = papers.shape[0]
    ext = rows + 2 * RIM
    column = lax.broadcasted_iota(jnp.int32, (ext, rows), 0)
    picks = jnp.zeros((ext, rows), F32)
    for which in range(K_CIT):
        picks = picks + (column == cite[which : which + 1, :]).astype(F32)
    picks = picks.astype(BF)
    cites = mm(picks[:RIM], low[...], TN)
    cites = cites + mm(picks[RIM : RIM + rows], papers[...], TN)
    cites = cites + mm(picks[RIM + rows :], high[...], TN)
    cite_agg = (cites * (1.0 / K_CIT)).astype(BF)
    pre = mm(papers[...], w_self[...], NN)
    base[...] = pre + mm(cite_agg, w_cite[...], NN) + bias[...]


def node_kernel(arrived, base, cotangent, w_aut, updated, slot_grad):
    total = arrived.shape[0]
    rows = base.shape[0]
    width = w_aut.shape[0]
    aux = arrived[:, width:]
    row_of = aux[:, :1].astype(F32)
    wanted = lax.broadcasted_iota(jnp.int32, (total, rows), 1).astype(F32) + 1.0
    match = (row_of == wanted).astype(F32).astype(BF)
    messages = mm(arrived[:, :width], w_aut[...], NN).astype(BF)
    aut_sum = mm(match, messages, TN)
    count = mm(match, aux, TN)[:, 1:2]
    inverse = 1.0 / jnp.maximum(count, 1.0)
    pre = base[...] + aut_sum * inverse
    sigma = jax.nn.sigmoid(pre)
    updated[...] = (pre * sigma).astype(BF)
    delta = cotangent[...].astype(F32) * sigma * (1.0 + pre * (1.0 - sigma))
    scaled = (delta * inverse).astype(BF)
    slot_grad[...] = mm(match, scaled, NN).astype(BF)


def weight_kernel(arrived, slot_grad, partial):
    width = partial.shape[0]
    partial[...] = mm(arrived[:, :width], slot_grad[...], TN).astype(BF)


def author_kernel(returned, owner, w_aut, grad_authors):
    grad_proj = mm(owner[...], returned[...], TN).astype(BF)
    grad_authors[...] = mm(grad_proj, w_aut[...], NT).astype(BF)


def shift_sum(block, place, count, axis, perm, dim):
    size = block.shape[dim] // count

    def piece(at):
        start = [0] * block.ndim
        start[dim] = at * size
        sizes = list(block.shape)
        sizes[dim] = size
        return lax.dynamic_slice(block, start, sizes, allow_negative_indices=False)

    came = [
        lax.ppermute(piece(lax.rem(place + k, count)), axis, perm(k)) for k in range(1, count)
    ]
    total = piece(place).astype(F32)
    for other in came:
        total = total + other.astype(F32)
    return total


def reduce_weight(partial, grp_count, dev_count):
    side = math.isqrt(grp_count)
    low = 4
    grp = lax.axis_index("grp")
    dev = lax.axis_index("dev")
    x, y = lax.div(grp, side), lax.rem(grp, side)
    z_low, core = (dev >> 1) & (low - 1), dev & 1

    def along_x(k):
        return [(g, (g // side + k) % side * side + g % side) for g in range(grp_count)]

    def along_y(k):
        return [(g, g // side * side + (g % side + k) % side) for g in range(grp_count)]

    def along_core(k):
        return [(d, d ^ 1) for d in range(dev_count)]

    def along_low(k):
        span = 2 * low
        return [(d, d // span * span + (d + 2 * k) % span) for d in range(dev_count)]

    part = shift_sum(partial, x, side, "grp", along_x, 0).astype(BF)
    part = shift_sum(part, y, side, "grp", along_y, 0).astype(BF)
    part = shift_sum(part, core, 2, "dev", along_core, 0)
    part = shift_sum(part, z_low, low, "dev", along_low, 1)
    span = 2 * low
    far = [[b * span + i for b in range(dev_count // span)] for i in range(span)]
    near = [[b * span + i for i in range(span)] for b in range(dev_count // span)]
    rows, lanes = part.shape
    every = lax.all_gather(part, "dev", axis_index_groups=far, axis=0)
    part = jnp.sum(every, axis=0).astype(BF)
    near_all = lax.all_gather(part, "dev", axis_index_groups=near, axis=0)
    near_all = near_all.reshape(low, 2, rows, lanes).transpose(1, 2, 0, 3)
    near_all = near_all.reshape(2 * rows, low * lanes)
    return lax.all_gather(near_all, "grp", axis=0, tiled=True)


def per_device(
    papers,
    authors,
    cotangent,
    w_self,
    w_cite,
    w_aut,
    bias,
    cite_col,
    edge_author,
    edge_dest,
    edge_row,
):
    dev_count = lax.axis_size("dev")
    grp_count = lax.axis_size("grp")
    all_count = grp_count * dev_count
    pap_rows, width = papers.shape
    aut_rows = authors.shape[0]
    edges = edge_author.shape[0]
    slots = 2 * edges // dev_count
    total = dev_count * slots
    hidden = w_aut.shape[1]
    shape = jax.ShapeDtypeStruct

    outgoing, owner = call(
        functools.partial(pack_kernel, dev_count),
        (shape((total, width + AUX), BF), shape((total, aut_rows), BF)),
        (
            authors,
            edge_author.reshape(1, edges),
            edge_dest.reshape(1, edges),
            edge_row.reshape(1, edges),
        ),
        2 * total * aut_rows * (edges + width),
    )
    arrived = lax.all_to_all(
        outgoing.reshape(dev_count, slots, width + AUX), "dev", 0, 0, tiled=True
    ).reshape(total, width + AUX)
    forward = [(i, i + 1) for i in range(dev_count - 1)]
    backward = [(i + 1, i) for i in range(dev_count - 1)]
    low = lax.ppermute(papers[pap_rows - RIM :], "dev", forward)
    high = lax.ppermute(papers[:RIM], "dev", backward)
    (base,) = call(
        base_kernel,
        (shape((pap_rows, hidden), F32),),
        (papers, low, high, cite_col.T, w_self, w_cite, bias.reshape(1, hidden)),
        2 * pap_rows * width * (2 * hidden + pap_rows + 2 * RIM),
    )
    updated, slot_grad = call(
        node_kernel,
        (shape((pap_rows, hidden), BF), shape((total, hidden), BF)),
        (arrived, base, cotangent, w_aut),
        2 * total * hidden * (width + 2 * pap_rows),
    )
    returned = lax.all_to_all(
        slot_grad.reshape(dev_count, slots, hidden), "dev", 0, 0, tiled=True
    ).reshape(total, hidden)
    (partial,) = call(
        weight_kernel,
        (shape((width, hidden), BF),),
        (arrived, slot_grad),
        2 * total * width * hidden,
    )
    summed = reduce_weight(partial, grp_count, dev_count)
    (grad_authors,) = call(
        author_kernel,
        (shape((aut_rows, width), BF),),
        (returned, owner, w_aut),
        2 * aut_rows * hidden * (total + width),
    )
    grad_w_aut = summed.astype(F32) / jnp.sqrt(jnp.float32(all_count * aut_rows))
    return (updated, grad_authors, grad_w_aut)


def solution(mesh):
    placed = (
        P(("grp", "dev"), None),
        P(("grp", "dev"), None),
        P(("grp", "dev"), None),
        P(),
        P(),
        P(),
        P(),
        P(("grp", "dev"), None),
        P(("grp", "dev")),
        P(("grp", "dev"), None),
        P(("grp", "dev")),
    )
    return jax.shard_map(
        per_device,
        mesh=mesh,
        in_specs=placed,
        out_specs=(P(("grp", "dev"), None), P(("grp", "dev"), None), P()),
        check_vma=False,
    )
```

```python
import functools
import math

import jax
import jax.numpy as jnp
from jax import lax
from jax.experimental import pallas as pl
from jax.experimental.pallas import tpu as pltpu
from jax.sharding import PartitionSpec as P

RIM = 64
K_CIT = 8
AUX = 128
HALVES = 2
NEAR = 4
BF = jnp.bfloat16
F32 = jnp.float32
NN = (((1,), (0,)), ((), ()))
NT = (((1,), (1,)), ((), ()))
TN = (((0,), (0,)), ((), ()))


def mm(a, b, dims):
    return lax.dot_general(a, b, dims, preferred_element_type=F32)


def where_equal(a, b):
    return (a == b).astype(F32).astype(BF)


def iota(shape, dim):
    return lax.broadcasted_iota(jnp.int32, shape, dim)


def call(kernel, outs, args, flops):
    moved = sum(math.prod(a.shape) * a.dtype.itemsize for a in list(args) + list(outs))
    return pl.pallas_call(
        kernel,
        out_shape=outs,
        compiler_params=pltpu.CompilerParams(vmem_limit_bytes=16 * 1024 * 1024),
        cost_estimate=pl.CostEstimate(flops=flops, bytes_accessed=moved, transcendentals=0),
    )(*args)


def edge_slots(dest_of, devs, cap):
    edges = dest_of.shape[1]
    hot = (iota((devs, edges), 0) == dest_of).astype(F32)
    before = (iota((edges, edges), 0) < iota((edges, edges), 1)).astype(F32).astype(BF)
    earlier = mm(hot.astype(BF), before, NN)
    rank = jnp.sum(hot * earlier, axis=0, keepdims=True)
    return dest_of * cap + rank.astype(jnp.int32)


def pack_kernel(devs, cap, authors, ends, out):
    auts, width = authors.shape
    edges = ends.shape[1]
    lines = out.shape[0]
    side = cap // HALVES
    position = edge_slots(ends[0:1, :], devs, cap)
    author_edge = where_equal(iota((auts, edges), 0), ends[1:2, :])
    rows = ends[2:3, :] + 1
    lane = iota((AUX, edges), 0)
    line = iota((lines, edges), 0) * side
    picked, aux = [], jnp.zeros((lines, AUX), F32)
    for q in range(side):
        slot_edge = where_equal(line + q, position)
        picked.append(mm(slot_edge, author_edge, NT).astype(BF))
        aux = aux + mm(slot_edge, jnp.where(lane == q, rows, 0).astype(F32).astype(BF), NT)
    out[:, side * width :] = aux.astype(BF)
    for q in range(side):
        out[:, q * width : (q + 1) * width] = mm(picked[q], authors[...], NN).astype(BF)


def base_kernel(devs, cap, papers, low, high, cite, w_self, w_cite, bias, ends, base, owner):
    rows = papers.shape[0]
    ext = rows + 2 * RIM
    column = iota((ext, rows), 0)
    picks = jnp.zeros((ext, rows), F32)
    for which in range(K_CIT):
        picks = picks + (column == cite[which : which + 1, :]).astype(F32)
    picks = picks.astype(BF)
    cites = mm(picks[:RIM], low[...], TN)
    cites = cites + mm(picks[RIM : RIM + rows], papers[...], TN)
    cites = cites + mm(picks[RIM + rows :], high[...], TN)
    cite_agg = (cites * (1.0 / K_CIT)).astype(BF)
    pre = mm(papers[...], w_self[...], NN)
    base[...] = pre + mm(cite_agg, w_cite[...], NN) + bias[...]
    total, auts = owner.shape
    edges = ends.shape[1]
    slot_edge = where_equal(iota((total, edges), 0), edge_slots(ends[0:1, :], devs, cap))
    author_edge = where_equal(iota((auts, edges), 0), ends[1:2, :])
    owner[...] = mm(slot_edge, author_edge, NT).astype(BF)


def split_match(arrived, width, rows):
    lines = arrived.shape[0]
    side = (arrived.shape[1] - AUX) // width
    aux = arrived[:, side * width :].astype(F32)
    wanted = iota((lines, rows), 1).astype(F32) + 1.0
    match = [where_equal(aux[:, q : q + 1], wanted) for q in range(side)]
    return jnp.concatenate(match, axis=0), aux


def side_rows(arrived, width):
    side = (arrived.shape[1] - AUX) // width
    return jnp.concatenate(
        [arrived[:, q * width : (q + 1) * width] for q in range(side)], axis=0
    )


def node_kernel(arrived, base, cotangent, w_aut, updated, slot_grad, scaled_out):
    width = w_aut.shape[0]
    rows = base.shape[0]
    total = slot_grad.shape[0]
    lines = arrived.shape[0]
    side = total // lines
    match, aux = split_match(arrived, width, rows)
    messages = mm(side_rows(arrived, width), w_aut[...], NN).astype(BF)
    aut_sum = mm(match, messages, TN)
    count = mm(match, jnp.ones((total, AUX), BF), TN)[:, :1]
    inverse = 1.0 / jnp.maximum(count, 1.0)
    pre = base[...] + aut_sum * inverse
    sigma = jax.nn.sigmoid(pre)
    updated[...] = (pre * sigma).astype(BF)
    delta = cotangent[...].astype(F32) * sigma * (1.0 + pre * (1.0 - sigma))
    scaled = (delta * inverse).astype(BF)
    scaled_out[...] = scaled
    spread = where_equal(iota((total, lines), 0) // side, iota((total, lines), 1))
    lanes = mm(spread, aux.astype(BF), NN)
    own_lane = iota((total, AUX), 1) == iota((total, AUX), 0) % side
    row_of = jnp.sum(jnp.where(own_lane, lanes, 0.0), axis=1, keepdims=True)
    slot_match = where_equal(row_of, iota((total, rows), 1).astype(F32) + 1.0)
    slot_grad[...] = mm(slot_match, scaled, NN).astype(BF)


def weight_kernel(arrived, scaled, partial):
    width = partial.shape[0]
    match, _ = split_match(arrived, width, scaled.shape[0])
    grads = mm(match, scaled[...], NN).astype(BF)
    partial[...] = mm(side_rows(arrived, width), grads, TN).astype(BF)


def author_kernel(returned, owner, w_aut, grad_authors):
    grad_proj = mm(owner[...], returned[...], TN).astype(BF)
    grad_authors[...] = mm(grad_proj, w_aut[...], NT).astype(BF)


def spread_kernel(scale, side, blocks, out):
    count, rows, lanes = blocks.shape
    near = count // (side * side)
    halves = near // 2
    for n in range(count):
        group, place = n // near, n % near
        core, z = place % 2, place // 2
        at = (core * side * side + group) * rows
        column = 0
        for bit in range(halves.bit_length() - 1):
            column = column * 2 + (z >> bit & 1)
        out[at : at + rows, column * lanes : (column + 1) * lanes] = blocks[n].astype(F32) * scale


def shift_sum(block, place, count, axis, perm):
    size = block.shape[0] // count

    def piece(at):
        return lax.dynamic_slice(
            block, (at * size, 0), (size, block.shape[1]), allow_negative_indices=False
        )

    came = [
        lax.ppermute(piece(lax.rem(place + k, count)), axis, perm(k)) for k in range(1, count)
    ]
    total = piece(place).astype(F32)
    for other in came:
        total = total + other.astype(F32)
    return total


def half_sum(block, bit, axis, perm):
    size = block.shape[1] // 2

    def piece(at):
        return lax.dynamic_slice(
            block, (0, at * size), (block.shape[0], size), allow_negative_indices=False
        )

    came = lax.ppermute(piece(1 - bit), axis, perm)
    return piece(bit).astype(F32) + came.astype(F32)


def reduce_weight(partial, grp_count, dev_count):
    side = math.isqrt(grp_count)
    grp = lax.axis_index("grp")
    dev = lax.axis_index("dev")
    x, y = lax.div(grp, side), lax.rem(grp, side)

    def along_x(k):
        return [(g, (g // side + k) % side * side + g % side) for g in range(grp_count)]

    def along_y(k):
        return [(g, g // side * side + (g % side + k) % side) for g in range(grp_count)]

    def along_dev(k):
        return [(d, d ^ k) for d in range(dev_count)]

    part = shift_sum(partial, dev & 1, 2, "dev", lambda k: along_dev(k)).astype(BF)
    part = shift_sum(part, x, side, "grp", along_x).astype(BF)
    part = shift_sum(part, y, side, "grp", along_y)
    step = 2
    while step < 2 * NEAR:
        part = half_sum(part, jnp.where(dev & step, 1, 0), "dev", along_dev(step))
        step = step * 2
    far = [list(range(i, dev_count, step)) for i in range(step)]
    part = jnp.sum(lax.all_gather(part, "dev", axis_index_groups=far, axis=0), axis=0)
    return part.astype(BF)


def gather_weight(part, grp_count, dev_count, scale):
    near = 2 * NEAR
    rows, lanes = part.shape
    groups = [[b * near + i for i in range(near)] for b in range(dev_count // near)]
    part = lax.all_to_all(
        jnp.broadcast_to(part[None], (near, rows, lanes)),
        "dev",
        0,
        0,
        axis_index_groups=groups,
        tiled=True,
    )
    blocks = lax.all_to_all(
        jnp.broadcast_to(part[None], (grp_count, near, rows, lanes)), "grp", 0, 0, tiled=True
    ).reshape(grp_count * near, rows, lanes)
    side = math.isqrt(grp_count)
    shape = jax.ShapeDtypeStruct((2 * grp_count * rows, NEAR * lanes), F32)
    (whole,) = call(functools.partial(spread_kernel, scale, side), (shape,), (blocks,), 0)
    return whole


def per_device(
    papers,
    authors,
    cotangent,
    w_self,
    w_cite,
    w_aut,
    bias,
    cite_col,
    edge_author,
    edge_dest,
    edge_row,
):
    dev_count = lax.axis_size("dev")
    grp_count = lax.axis_size("grp")
    pap_rows, width = papers.shape
    aut_rows = authors.shape[0]
    edges = edge_author.shape[0]
    slots = 2 * edges // dev_count
    total = dev_count * slots
    hidden = w_aut.shape[1]
    lines = dev_count * HALVES
    line = slots // HALVES * width + AUX
    shape = jax.ShapeDtypeStruct
    ends = jnp.stack([edge_dest[:, 0], edge_author, edge_row])

    (outgoing,) = call(
        functools.partial(pack_kernel, dev_count, slots),
        (shape((lines, line), BF),),
        (authors, ends),
        2 * total * aut_rows * (edges + width),
    )
    arrived = lax.all_to_all(
        outgoing.reshape(dev_count, HALVES, line), "dev", 0, 0, tiled=True
    ).reshape(lines, line)
    forward = [(i, i + 1) for i in range(dev_count - 1)]
    backward = [(i + 1, i) for i in range(dev_count - 1)]
    low = lax.ppermute(papers[pap_rows - RIM :], "dev", forward)
    high = lax.ppermute(papers[:RIM], "dev", backward)
    base, owner = call(
        functools.partial(base_kernel, dev_count, slots),
        (shape((pap_rows, hidden), F32), shape((total, aut_rows), BF)),
        (papers, low, high, cite_col.T, w_self, w_cite, bias.reshape(1, hidden), ends),
        2 * pap_rows * width * (2 * hidden + pap_rows + 2 * RIM),
    )
    updated, slot_grad, scaled = call(
        node_kernel,
        (
            shape((pap_rows, hidden), BF),
            shape((total, hidden), BF),
            shape((pap_rows, hidden), BF),
        ),
        (arrived, base, cotangent, w_aut),
        2 * total * hidden * (width + 2 * pap_rows),
    )
    returned = lax.all_to_all(
        slot_grad.reshape(dev_count, slots, hidden), "dev", 0, 0, tiled=True
    ).reshape(total, hidden)
    (partial,) = call(
        weight_kernel,
        (shape((width, hidden), BF),),
        (arrived, scaled),
        2 * total * width * hidden,
    )
    part = reduce_weight(partial, grp_count, dev_count)
    part, returned = lax.optimization_barrier((part, returned))
    (grad_authors,) = call(
        author_kernel,
        (shape((aut_rows, width), BF),),
        (returned, owner, w_aut),
        2 * aut_rows * hidden * (total + width),
    )
    scale = 1.0 / math.sqrt(grp_count * dev_count * aut_rows)
    grad_w_aut = gather_weight(part, grp_count, dev_count, scale)
    return (updated, grad_authors, grad_w_aut)


def solution(mesh):
    placed = (
        P(("grp", "dev"), None),
        P(("grp", "dev"), None),
        P(("grp", "dev"), None),
        P(),
        P(),
        P(),
        P(),
        P(("grp", "dev"), None),
        P(("grp", "dev")),
        P(("grp", "dev"), None),
        P(("grp", "dev")),
    )
    return jax.shard_map(
        per_device,
        mesh=mesh,
        in_specs=placed,
        out_specs=(P(("grp", "dev"), None), P(("grp", "dev"), None), P()),
        check_vma=False,
    )
```

```python
import functools
import math

import jax
import jax.numpy as jnp
from jax import lax
from jax.experimental import pallas as pl
from jax.experimental.pallas import tpu as pltpu
from jax.sharding import PartitionSpec as P

RIM = 64
K_CIT = 8
AUX = 128
HALVES = 2
BF = jnp.bfloat16
F32 = jnp.float32
NN = (((1,), (0,)), ((), ()))
NT = (((1,), (1,)), ((), ()))
TN = (((0,), (0,)), ((), ()))


def mm(a, b, dims):
    return lax.dot_general(a, b, dims, preferred_element_type=F32)


def where_equal(a, b):
    return (a == b).astype(F32).astype(BF)


def iota(shape, dim):
    return lax.broadcasted_iota(jnp.int32, shape, dim)


def call(kernel, outs, args, flops):
    moved = sum(math.prod(a.shape) * a.dtype.itemsize for a in list(args) + list(outs))
    return pl.pallas_call(
        kernel,
        out_shape=outs,
        compiler_params=pltpu.CompilerParams(vmem_limit_bytes=16 * 1024 * 1024),
        cost_estimate=pl.CostEstimate(flops=flops, bytes_accessed=moved, transcendentals=0),
    )(*args)


def edge_slots(dest_of, devs, cap):
    edges = dest_of.shape[1]
    hot = (iota((devs, edges), 0) == dest_of).astype(F32)
    before = (iota((edges, edges), 0) < iota((edges, edges), 1)).astype(F32).astype(BF)
    earlier = mm(hot.astype(BF), before, NN)
    rank = jnp.sum(hot * earlier, axis=0, keepdims=True)
    return dest_of * cap + rank.astype(jnp.int32)


def pack_kernel(devs, cap, authors, ends, out):
    auts, width = authors.shape
    edges = ends.shape[1]
    lines = out.shape[0]
    side = cap // HALVES
    position = edge_slots(ends[0:1, :], devs, cap)
    author_edge = where_equal(iota((auts, edges), 0), ends[1:2, :])
    rows = ends[2:3, :] + 1
    lane = iota((AUX, edges), 0)
    line = iota((lines, edges), 0) * side
    picked, aux = [], jnp.zeros((lines, AUX), F32)
    for q in range(side):
        slot_edge = where_equal(line + q, position)
        picked.append(mm(slot_edge, author_edge, NT).astype(BF))
        aux = aux + mm(slot_edge, jnp.where(lane == q, rows, 0).astype(F32).astype(BF), NT)
    out[:, side * width :] = aux.astype(BF)
    for q in range(side):
        out[:, q * width : (q + 1) * width] = mm(picked[q], authors[...], NN).astype(BF)


def base_kernel(devs, cap, papers, low, high, cite, w_self, w_cite, bias, ends, base, owner):
    rows = papers.shape[0]
    ext = rows + 2 * RIM
    column = iota((ext, rows), 0)
    picks = jnp.zeros((ext, rows), F32)
    for which in range(K_CIT):
        picks = picks + (column == cite[which : which + 1, :]).astype(F32)
    picks = picks.astype(BF)
    cites = mm(picks[:RIM], low[...], TN)
    cites = cites + mm(picks[RIM : RIM + rows], papers[...], TN)
    cites = cites + mm(picks[RIM + rows :], high[...], TN)
    cite_agg = (cites * (1.0 / K_CIT)).astype(BF)
    pre = mm(papers[...], w_self[...], NN)
    base[...] = pre + mm(cite_agg, w_cite[...], NN) + bias[...]
    total, auts = owner.shape
    edges = ends.shape[1]
    slot_edge = where_equal(iota((total, edges), 0), edge_slots(ends[0:1, :], devs, cap))
    author_edge = where_equal(iota((auts, edges), 0), ends[1:2, :])
    owner[...] = mm(slot_edge, author_edge, NT).astype(BF)


def split_match(arrived, width, rows):
    lines = arrived.shape[0]
    side = (arrived.shape[1] - AUX) // width
    aux = arrived[:, side * width :].astype(F32)
    wanted = iota((lines, rows), 1).astype(F32) + 1.0
    match = [where_equal(aux[:, q : q + 1], wanted) for q in range(side)]
    return jnp.concatenate(match, axis=0), aux


def side_rows(arrived, width):
    side = (arrived.shape[1] - AUX) // width
    return jnp.concatenate(
        [arrived[:, q * width : (q + 1) * width] for q in range(side)], axis=0
    )


def node_kernel(arrived, base, cotangent, w_aut, updated, slot_grad, scaled_out):
    width = w_aut.shape[0]
    rows = base.shape[0]
    total = slot_grad.shape[0]
    lines = arrived.shape[0]
    side = total // lines
    match, aux = split_match(arrived, width, rows)
    messages = mm(side_rows(arrived, width), w_aut[...], NN).astype(BF)
    aut_sum = mm(match, messages, TN)
    count = mm(match, jnp.ones((total, AUX), BF), TN)[:, :1]
    inverse = 1.0 / jnp.maximum(count, 1.0)
    pre = base[...] + aut_sum * inverse
    sigma = jax.nn.sigmoid(pre)
    updated[...] = (pre * sigma).astype(BF)
    delta = cotangent[...].astype(F32) * sigma * (1.0 + pre * (1.0 - sigma))
    scaled = (delta * inverse).astype(BF)
    scaled_out[...] = scaled
    spread = where_equal(iota((total, lines), 0) // side, iota((total, lines), 1))
    lanes = mm(spread, aux.astype(BF), NN)
    own_lane = iota((total, AUX), 1) == iota((total, AUX), 0) % side
    row_of = jnp.sum(jnp.where(own_lane, lanes, 0.0), axis=1, keepdims=True)
    slot_match = where_equal(row_of, iota((total, rows), 1).astype(F32) + 1.0)
    slot_grad[...] = mm(slot_match, scaled, NN).astype(BF)


def weight_kernel(arrived, scaled, partial):
    width = partial.shape[0]
    match, _ = split_match(arrived, width, scaled.shape[0])
    grads = mm(match, scaled[...], NN).astype(BF)
    partial[...] = mm(side_rows(arrived, width), grads, TN).astype(BF)


def author_kernel(returned, owner, w_aut, grad_authors):
    grad_proj = mm(owner[...], returned[...], TN).astype(BF)
    grad_authors[...] = mm(grad_proj, w_aut[...], NT).astype(BF)


def ring_kernel(every, out):
    total = every[0].astype(F32)
    for n in range(1, every.shape[0]):
        total = total + every[n].astype(F32)
    total = total.astype(BF)
    for n in range(out.shape[0]):
        out[n] = total


def spread_kernel(scale, own, other, core, out):
    half = own.shape[0]
    first = core[0] == 0
    mine, came = own[...].astype(F32) * scale, other[...].astype(F32) * scale
    out[:half, :] = jnp.where(first, mine, came)
    out[half:, :] = jnp.where(first, came, mine)


def shift_sum(block, place, count, axis, perm):
    size = block.shape[0] // count

    def piece(at):
        return lax.dynamic_slice(
            block, (at * size, 0), (size, block.shape[1]), allow_negative_indices=False
        )

    came = [
        lax.ppermute(piece(lax.rem(place + k, count)), axis, perm(k)) for k in range(1, count)
    ]
    total = piece(place).astype(F32)
    for other in came:
        total = total + other.astype(F32)
    return total


def swap(block):
    return lax.ppermute(block, "dev", [(d, d ^ 1) for d in range(lax.axis_size("dev"))])


def reduce_weight(partial, grp_count, dev_count):
    side = math.isqrt(grp_count)
    grp = lax.axis_index("grp")
    core = lax.axis_index("dev") & 1
    x, y = lax.div(grp, side), lax.rem(grp, side)

    def along_x(k):
        return [(g, (g // side + k) % side * side + g % side) for g in range(grp_count)]

    def along_y(k):
        return [(g, g // side * side + (g % side + k) % side) for g in range(grp_count)]

    def along_core(k):
        return [(d, d ^ k) for d in range(dev_count)]

    part = shift_sum(partial, core, 2, "dev", along_core).astype(BF)
    part = shift_sum(part, x, side, "grp", along_x).astype(BF)
    part = shift_sum(part, y, side, "grp", along_y).astype(BF)
    ring = [list(range(i, dev_count, 2)) for i in range(2)]
    every = lax.all_gather(part, "dev", axis_index_groups=ring, axis=0)
    copies = jax.ShapeDtypeStruct((grp_count, *part.shape), BF)
    (out,) = call(ring_kernel, (copies,), (every,), 0)
    return out


def gather_weight(copies, scale):
    grp_count, rows, lanes = copies.shape
    own = lax.all_to_all(copies, "grp", 0, 0, tiled=True).reshape(grp_count * rows, lanes)
    other = swap(own)
    core = (lax.axis_index("dev") & 1).reshape(1)
    whole = pl.pallas_call(
        functools.partial(spread_kernel, scale),
        out_shape=jax.ShapeDtypeStruct((2 * grp_count * rows, lanes), F32),
        in_specs=[
            pl.BlockSpec(memory_space=pltpu.VMEM),
            pl.BlockSpec(memory_space=pltpu.VMEM),
            pl.BlockSpec(memory_space=pltpu.SMEM),
        ],
        compiler_params=pltpu.CompilerParams(vmem_limit_bytes=16 * 1024 * 1024),
    )(own, other, core)
    return whole


def per_device(
    papers,
    authors,
    cotangent,
    w_self,
    w_cite,
    w_aut,
    bias,
    cite_col,
    edge_author,
    edge_dest,
    edge_row,
):
    dev_count = lax.axis_size("dev")
    grp_count = lax.axis_size("grp")
    pap_rows, width = papers.shape
    aut_rows = authors.shape[0]
    edges = edge_author.shape[0]
    slots = 2 * edges // dev_count
    total = dev_count * slots
    hidden = w_aut.shape[1]
    lines = dev_count * HALVES
    line = slots // HALVES * width + AUX
    shape = jax.ShapeDtypeStruct
    ends = jnp.stack([edge_dest[:, 0], edge_author, edge_row])

    (outgoing,) = call(
        functools.partial(pack_kernel, dev_count, slots),
        (shape((lines, line), BF),),
        (authors, ends),
        2 * total * aut_rows * (edges + width),
    )
    arrived = lax.all_to_all(
        outgoing.reshape(dev_count, HALVES, line), "dev", 0, 0, tiled=True
    ).reshape(lines, line)
    forward = [(i, i + 1) for i in range(dev_count - 1)]
    backward = [(i + 1, i) for i in range(dev_count - 1)]
    low = lax.ppermute(papers[pap_rows - RIM :], "dev", forward)
    high = lax.ppermute(papers[:RIM], "dev", backward)
    base, owner = call(
        functools.partial(base_kernel, dev_count, slots),
        (shape((pap_rows, hidden), F32), shape((total, aut_rows), BF)),
        (papers, low, high, cite_col.T, w_self, w_cite, bias.reshape(1, hidden), ends),
        2 * pap_rows * width * (2 * hidden + pap_rows + 2 * RIM),
    )
    updated, slot_grad, scaled = call(
        node_kernel,
        (
            shape((pap_rows, hidden), BF),
            shape((total, hidden), BF),
            shape((pap_rows, hidden), BF),
        ),
        (arrived, base, cotangent, w_aut),
        2 * total * hidden * (width + 2 * pap_rows),
    )
    returned = lax.all_to_all(
        slot_grad.reshape(dev_count, slots, hidden), "dev", 0, 0, tiled=True
    ).reshape(total, hidden)
    (partial,) = call(
        weight_kernel,
        (shape((width, hidden), BF),),
        (arrived, scaled),
        2 * total * width * hidden,
    )
    part = reduce_weight(partial, grp_count, dev_count)
    part, returned = lax.optimization_barrier((part, returned))
    (grad_authors,) = call(
        author_kernel,
        (shape((aut_rows, width), BF),),
        (returned, owner, w_aut),
        2 * aut_rows * hidden * (total + width),
    )
    scale = 1.0 / math.sqrt(grp_count * dev_count * aut_rows)
    grad_w_aut = gather_weight(part, scale)
    return (updated, grad_authors, grad_w_aut)


def solution(mesh):
    placed = (
        P(("grp", "dev"), None),
        P(("grp", "dev"), None),
        P(("grp", "dev"), None),
        P(),
        P(),
        P(),
        P(),
        P(("grp", "dev"), None),
        P(("grp", "dev")),
        P(("grp", "dev"), None),
        P(("grp", "dev")),
    )
    return jax.shard_map(
        per_device,
        mesh=mesh,
        in_specs=placed,
        out_specs=(P(("grp", "dev"), None), P(("grp", "dev"), None), P()),
        check_vma=False,
    )
```

```python
import functools
import math

import jax
import jax.numpy as jnp
from jax import lax
from jax.experimental import pallas as pl
from jax.experimental.pallas import tpu as pltpu
from jax.sharding import PartitionSpec as P

RIM = 64
K_CIT = 8
AUX = 128
HALVES = 2
NEAR = 4
BF = jnp.bfloat16
F32 = jnp.float32
NN = (((1,), (0,)), ((), ()))
NT = (((1,), (1,)), ((), ()))
TN = (((0,), (0,)), ((), ()))


def mm(a, b, dims):
    return lax.dot_general(a, b, dims, preferred_element_type=F32)


def where_equal(a, b):
    return (a == b).astype(F32).astype(BF)


def iota(shape, dim):
    return lax.broadcasted_iota(jnp.int32, shape, dim)


def call(kernel, outs, args, flops):
    moved = sum(math.prod(a.shape) * a.dtype.itemsize for a in list(args) + list(outs))
    return pl.pallas_call(
        kernel,
        out_shape=outs,
        compiler_params=pltpu.CompilerParams(vmem_limit_bytes=16 * 1024 * 1024),
        cost_estimate=pl.CostEstimate(flops=flops, bytes_accessed=moved, transcendentals=0),
    )(*args)


def edge_slots(dest_of, devs, cap):
    edges = dest_of.shape[1]
    hot = (iota((devs, edges), 0) == dest_of).astype(F32)
    before = (iota((edges, edges), 0) < iota((edges, edges), 1)).astype(F32).astype(BF)
    earlier = mm(hot.astype(BF), before, NN)
    rank = jnp.sum(hot * earlier, axis=0, keepdims=True)
    return dest_of * cap + rank.astype(jnp.int32)


def pack_kernel(devs, cap, authors, ends, out):
    auts, width = authors.shape
    edges = ends.shape[1]
    lines = out.shape[0] * out.shape[1]
    side = cap // HALVES
    position = edge_slots(ends[0:1, :], devs, cap)
    author_edge = where_equal(iota((auts, edges), 0), ends[1:2, :])
    rows = ends[2:3, :] + 1
    lane = iota((AUX, edges), 0)
    line = iota((lines, edges), 0) * side
    picked, aux = [], jnp.zeros((lines, AUX), F32)
    for q in range(side):
        slot_edge = where_equal(line + q, position)
        picked.append(mm(slot_edge, author_edge, NT).astype(BF))
        aux = aux + mm(slot_edge, jnp.where(lane == q, rows, 0).astype(F32).astype(BF), NT)
    out[:, :, side * width :] = aux.astype(BF).reshape(out.shape[0], HALVES, AUX)
    for q in range(side):
        rows_of = mm(picked[q], authors[...], NN).astype(BF)
        out[:, :, q * width : (q + 1) * width] = rows_of.reshape(out.shape[0], HALVES, width)


def base_kernel(devs, cap, papers, low, high, cite, w_self, w_cite, bias, ends, base, owner):
    rows = papers.shape[0]
    ext = rows + 2 * RIM
    column = iota((ext, rows), 0)
    picks = jnp.zeros((ext, rows), F32)
    for which in range(K_CIT):
        picks = picks + (column == cite[which : which + 1, :]).astype(F32)
    picks = picks.astype(BF)
    cites = mm(picks[:RIM], low[...], TN)
    cites = cites + mm(picks[RIM : RIM + rows], papers[...], TN)
    cites = cites + mm(picks[RIM + rows :], high[...], TN)
    cite_agg = (cites * (1.0 / K_CIT)).astype(BF)
    pre = mm(papers[...], w_self[...], NN)
    base[...] = pre + mm(cite_agg, w_cite[...], NN) + bias[...]
    total, auts = owner.shape
    edges = ends.shape[1]
    slot_edge = where_equal(iota((total, edges), 0), edge_slots(ends[0:1, :], devs, cap))
    author_edge = where_equal(iota((auts, edges), 0), ends[1:2, :])
    owner[...] = mm(slot_edge, author_edge, NT).astype(BF)


def split_match(aux, side, rows):
    lines = aux.shape[0]
    wanted = iota((lines, rows), 1).astype(F32) + 1.0
    match = [where_equal(aux[:, q : q + 1], wanted) for q in range(side)]
    return jnp.concatenate(match, axis=0)


def node_kernel(arrived, base, cotangent, w_aut, updated, slot_grad, side_rows, side_grad):
    width = w_aut.shape[0]
    rows = base.shape[0]
    total = slot_grad.shape[0]
    lines = arrived.shape[0] * arrived.shape[1]
    side = total // lines
    aux = arrived[:, :, side * width :].reshape(lines, AUX).astype(F32)
    match = split_match(aux, side, rows)
    for q in range(side):
        piece = arrived[:, :, q * width : (q + 1) * width].reshape(lines, width)
        side_rows[q * lines : (q + 1) * lines, :] = piece
    messages = mm(side_rows[...], w_aut[...], NN).astype(BF)
    aut_sum = mm(match, messages, TN)
    count = mm(match, jnp.ones((total, AUX), BF), TN)[:, :1]
    inverse = 1.0 / jnp.maximum(count, 1.0)
    pre = base[...] + aut_sum * inverse
    sigma = jax.nn.sigmoid(pre)
    updated[...] = (pre * sigma).astype(BF)
    delta = cotangent[...].astype(F32) * sigma * (1.0 + pre * (1.0 - sigma))
    scaled = (delta * inverse).astype(BF)
    side_grad[...] = mm(match, scaled, NN).astype(BF)
    spread = where_equal(iota((total, lines), 0) // side, iota((total, lines), 1))
    lanes = mm(spread, aux.astype(BF), NN)
    own_lane = iota((total, AUX), 1) == iota((total, AUX), 0) % side
    row_of = jnp.sum(jnp.where(own_lane, lanes, 0.0), axis=1, keepdims=True)
    slot_match = where_equal(row_of, iota((total, rows), 1).astype(F32) + 1.0)
    slot_grad[...] = mm(slot_match, scaled, NN).astype(BF)


def weight_kernel(side_rows, side_grad, partial):
    partial[...] = mm(side_rows[...], side_grad[...], TN).astype(BF)


def author_kernel(returned, owner, w_aut, grad_authors):
    grad_proj = mm(owner[...], returned[...], TN).astype(BF)
    grad_authors[...] = mm(grad_proj, w_aut[...], NT).astype(BF)


def sum_kernel(parts, copies):
    total = parts[0].astype(F32)
    for n in range(1, parts.shape[0]):
        total = total + parts[n].astype(F32)
    total = total.astype(BF)
    for n in range(copies.shape[0]):
        copies[n] = total


def copy_kernel(parts, copies):
    for n in range(copies.shape[0]):
        copies[n] = parts[...]


def spread_kernel(scale, side, blocks, out):
    count, rows, lanes = blocks.shape
    near = count // (side * side)
    halves = near // 2
    for n in range(count):
        group, place = n // near, n % near
        core, z = place % 2, place // 2
        at = (core * side * side + group) * rows
        column = 0
        for bit in range(halves.bit_length() - 1):
            column = column * 2 + (z >> bit & 1)
        out[at : at + rows, column * lanes : (column + 1) * lanes] = blocks[n].astype(F32) * scale


def shift_sum(block, place, count, axis, perm):
    size = block.shape[0] // count

    def piece(at):
        return lax.dynamic_slice(
            block, (at * size, 0), (size, block.shape[1]), allow_negative_indices=False
        )

    came = [
        lax.ppermute(piece(lax.rem(place + k, count)), axis, perm(k)) for k in range(1, count)
    ]
    total = piece(place).astype(F32)
    for other in came:
        total = total + other.astype(F32)
    return total


def half_sum(block, bit, axis, perm):
    size = block.shape[1] // 2

    def piece(at):
        return lax.dynamic_slice(
            block, (0, at * size), (block.shape[0], size), allow_negative_indices=False
        )

    came = lax.ppermute(piece(1 - bit), axis, perm)
    return piece(bit).astype(F32) + came.astype(F32)


def reduce_weight(partial, grp_count, dev_count):
    side = math.isqrt(grp_count)
    grp = lax.axis_index("grp")
    dev = lax.axis_index("dev")
    x, y = lax.div(grp, side), lax.rem(grp, side)

    def along_x(k):
        return [(g, (g // side + k) % side * side + g % side) for g in range(grp_count)]

    def along_y(k):
        return [(g, g // side * side + (g % side + k) % side) for g in range(grp_count)]

    def along_dev(k):
        return [(d, d ^ k) for d in range(dev_count)]

    part = shift_sum(partial, dev & 1, 2, "dev", lambda k: along_dev(k)).astype(BF)
    part = shift_sum(part, x, side, "grp", along_x).astype(BF)
    part = shift_sum(part, y, side, "grp", along_y)
    step = 2
    while step < 2 * NEAR:
        part = half_sum(part, jnp.where(dev & step, 1, 0), "dev", along_dev(step))
        step = step * 2
    return part.astype(BF)


def gather_weight(part, grp_count, dev_count, scale):
    near = 2 * NEAR
    far = dev_count // near
    rows, lanes = part.shape
    shape = jax.ShapeDtypeStruct
    apart = [list(range(i, dev_count, near)) for i in range(near)]
    beside = [[b * near + i for i in range(near)] for b in range(far)]

    def exchange(copies, axis, groups):
        return lax.all_to_all(copies, axis, 0, 0, axis_index_groups=groups, tiled=True)

    parts = exchange(jnp.broadcast_to(part[None], (far, rows, lanes)), "dev", apart)
    (copies,) = call(sum_kernel, (shape((near, rows, lanes), BF),), (parts,), 0)
    parts = exchange(copies, "dev", beside)
    (copies,) = call(copy_kernel, (shape((grp_count, near, rows, lanes), BF),), (parts,), 0)
    blocks = exchange(copies, "grp", None).reshape(grp_count * near, rows, lanes)
    side = math.isqrt(grp_count)
    whole_shape = shape((2 * grp_count * rows, NEAR * lanes), F32)
    (whole,) = call(functools.partial(spread_kernel, scale, side), (whole_shape,), (blocks,), 0)
    return whole


def per_device(
    papers,
    authors,
    cotangent,
    w_self,
    w_cite,
    w_aut,
    bias,
    cite_col,
    edge_author,
    edge_dest,
    edge_row,
):
    dev_count = lax.axis_size("dev")
    grp_count = lax.axis_size("grp")
    pap_rows, width = papers.shape
    aut_rows = authors.shape[0]
    edges = edge_author.shape[0]
    slots = 2 * edges // dev_count
    total = dev_count * slots
    hidden = w_aut.shape[1]
    lines = dev_count * HALVES
    line = slots // HALVES * width + AUX
    shape = jax.ShapeDtypeStruct
    ends = jnp.stack([edge_dest[:, 0], edge_author, edge_row])

    (outgoing,) = call(
        functools.partial(pack_kernel, dev_count, slots),
        (shape((dev_count, HALVES, line), BF),),
        (authors, ends),
        2 * total * aut_rows * (edges + width),
    )
    arrived = lax.all_to_all(
        outgoing, "dev", 0, 0, tiled=True
    )
    forward = [(i, i + 1) for i in range(dev_count - 1)]
    backward = [(i + 1, i) for i in range(dev_count - 1)]
    low = lax.ppermute(papers[pap_rows - RIM :], "dev", forward)
    high = lax.ppermute(papers[:RIM], "dev", backward)
    base, owner = call(
        functools.partial(base_kernel, dev_count, slots),
        (shape((pap_rows, hidden), F32), shape((total, aut_rows), BF)),
        (papers, low, high, cite_col.T, w_self, w_cite, bias.reshape(1, hidden), ends),
        2 * pap_rows * width * (2 * hidden + pap_rows + 2 * RIM),
    )
    updated, slot_grad, side_rows, side_grad = call(
        node_kernel,
        (
            shape((pap_rows, hidden), BF),
            shape((total, hidden), BF),
            shape((total, width), BF),
            shape((total, hidden), BF),
        ),
        (arrived, base, cotangent, w_aut),
        2 * total * hidden * (width + 2 * pap_rows),
    )
    returned = lax.all_to_all(
        slot_grad.reshape(dev_count, slots, hidden), "dev", 0, 0, tiled=True
    ).reshape(total, hidden)
    (partial,) = call(
        weight_kernel,
        (shape((width, hidden), BF),),
        (side_rows, side_grad),
        2 * total * width * hidden,
    )
    part = reduce_weight(partial, grp_count, dev_count)
    part, returned = lax.optimization_barrier((part, returned))
    (grad_authors,) = call(
        author_kernel,
        (shape((aut_rows, width), BF),),
        (returned, owner, w_aut),
        2 * aut_rows * hidden * (total + width),
    )
    scale = 1.0 / math.sqrt(grp_count * dev_count * aut_rows)
    grad_w_aut = gather_weight(part, grp_count, dev_count, scale)
    return (updated, grad_authors, grad_w_aut)


def solution(mesh):
    placed = (
        P(("grp", "dev"), None),
        P(("grp", "dev"), None),
        P(("grp", "dev"), None),
        P(),
        P(),
        P(),
        P(),
        P(("grp", "dev"), None),
        P(("grp", "dev")),
        P(("grp", "dev"), None),
        P(("grp", "dev")),
    )
    return jax.shard_map(
        per_device,
        mesh=mesh,
        in_specs=placed,
        out_specs=(P(("grp", "dev"), None), P(("grp", "dev"), None), P()),
        check_vma=False,
    )
```

```python
import functools
import math

import jax
import jax.numpy as jnp
from jax import lax
from jax.experimental import pallas as pl
from jax.experimental.pallas import tpu as pltpu
from jax.sharding import PartitionSpec as P

RIM = 64
K_CIT = 8
AUX = 128
HALVES = 2
BF = jnp.bfloat16
F32 = jnp.float32
NN = (((1,), (0,)), ((), ()))
NT = (((1,), (1,)), ((), ()))
TN = (((0,), (0,)), ((), ()))


def mm(a, b, dims):
    return lax.dot_general(a, b, dims, preferred_element_type=F32)


def where_equal(a, b):
    return (a == b).astype(F32).astype(BF)


def iota(shape, dim):
    return lax.broadcasted_iota(jnp.int32, shape, dim)


def call(kernel, outs, args, flops):
    moved = sum(math.prod(a.shape) * a.dtype.itemsize for a in list(args) + list(outs))
    return pl.pallas_call(
        kernel,
        out_shape=outs,
        compiler_params=pltpu.CompilerParams(vmem_limit_bytes=16 * 1024 * 1024),
        cost_estimate=pl.CostEstimate(flops=flops, bytes_accessed=moved, transcendentals=0),
    )(*args)


def edge_slots(dest_of, devs, cap):
    edges = dest_of.shape[1]
    hot = (iota((devs, edges), 0) == dest_of).astype(F32)
    before = (iota((edges, edges), 0) < iota((edges, edges), 1)).astype(F32).astype(BF)
    earlier = mm(hot.astype(BF), before, NN)
    rank = jnp.sum(hot * earlier, axis=0, keepdims=True)
    return dest_of * cap + rank.astype(jnp.int32)


def pack_kernel(devs, cap, authors, ends, out):
    auts, width = authors.shape
    edges = ends.shape[1]
    lines = out.shape[0] * out.shape[1]
    side = cap // HALVES
    position = edge_slots(ends[0:1, :], devs, cap)
    author_edge = where_equal(iota((auts, edges), 0), ends[1:2, :])
    rows = ends[2:3, :] + 1
    lane = iota((AUX, edges), 0)
    line = iota((lines, edges), 0) * side
    picked, aux = [], jnp.zeros((lines, AUX), F32)
    for q in range(side):
        slot_edge = where_equal(line + q, position)
        picked.append(mm(slot_edge, author_edge, NT).astype(BF))
        aux = aux + mm(slot_edge, jnp.where(lane == q, rows, 0).astype(F32).astype(BF), NT)
    out[:, :, side * width :] = aux.astype(BF).reshape(out.shape[0], HALVES, AUX)
    for q in range(side):
        rows_of = mm(picked[q], authors[...], NN).astype(BF)
        out[:, :, q * width : (q + 1) * width] = rows_of.reshape(out.shape[0], HALVES, width)


def base_kernel(devs, cap, papers, low, high, cite, w_self, w_cite, bias, ends, base, owner):
    rows = papers.shape[0]
    ext = rows + 2 * RIM
    column = iota((ext, rows), 0)
    picks = jnp.zeros((ext, rows), F32)
    for which in range(K_CIT):
        picks = picks + (column == cite[which : which + 1, :]).astype(F32)
    picks = picks.astype(BF)
    cites = mm(picks[:RIM], low[...], TN)
    cites = cites + mm(picks[RIM : RIM + rows], papers[...], TN)
    cites = cites + mm(picks[RIM + rows :], high[...], TN)
    cite_agg = (cites * (1.0 / K_CIT)).astype(BF)
    pre = mm(papers[...], w_self[...], NN)
    base[...] = pre + mm(cite_agg, w_cite[...], NN) + bias[...]
    total, auts = owner.shape
    edges = ends.shape[1]
    slot_edge = where_equal(iota((total, edges), 0), edge_slots(ends[0:1, :], devs, cap))
    author_edge = where_equal(iota((auts, edges), 0), ends[1:2, :])
    owner[...] = mm(slot_edge, author_edge, NT).astype(BF)


def split_match(aux, side, rows):
    lines = aux.shape[0]
    wanted = iota((lines, rows), 1).astype(F32) + 1.0
    match = [where_equal(aux[:, q : q + 1], wanted) for q in range(side)]
    return jnp.concatenate(match, axis=0)


def node_kernel(arrived, base, cotangent, w_aut, updated, slot_grad, side_rows, side_grad):
    width = w_aut.shape[0]
    rows = base.shape[0]
    total = slot_grad.shape[0]
    lines = arrived.shape[0] * arrived.shape[1]
    side = total // lines
    aux = arrived[:, :, side * width :].reshape(lines, AUX).astype(F32)
    match = split_match(aux, side, rows)
    for q in range(side):
        piece = arrived[:, :, q * width : (q + 1) * width].reshape(lines, width)
        side_rows[q * lines : (q + 1) * lines, :] = piece
    messages = mm(side_rows[...], w_aut[...], NN).astype(BF)
    aut_sum = mm(match, messages, TN)
    count = mm(match, jnp.ones((total, AUX), BF), TN)[:, :1]
    inverse = 1.0 / jnp.maximum(count, 1.0)
    pre = base[...] + aut_sum * inverse
    sigma = jax.nn.sigmoid(pre)
    updated[...] = (pre * sigma).astype(BF)
    delta = cotangent[...].astype(F32) * sigma * (1.0 + pre * (1.0 - sigma))
    scaled = (delta * inverse).astype(BF)
    side_grad[...] = mm(match, scaled, NN).astype(BF)
    spread = where_equal(iota((total, lines), 0) // side, iota((total, lines), 1))
    lanes = mm(spread, aux.astype(BF), NN)
    own_lane = iota((total, AUX), 1) == iota((total, AUX), 0) % side
    row_of = jnp.sum(jnp.where(own_lane, lanes, 0.0), axis=1, keepdims=True)
    slot_match = where_equal(row_of, iota((total, rows), 1).astype(F32) + 1.0)
    slot_grad[...] = mm(slot_match, scaled, NN).astype(BF)


def weight_kernel(side_rows, side_grad, partial):
    partial[...] = mm(side_rows[...], side_grad[...], TN).astype(BF)


def author_kernel(returned, owner, w_aut, grad_authors):
    grad_proj = mm(owner[...], returned[...], TN).astype(BF)
    grad_authors[...] = mm(grad_proj, w_aut[...], NT).astype(BF)


def ring_kernel(every, out):
    total = every[0].astype(F32)
    for n in range(1, every.shape[0]):
        total = total + every[n].astype(F32)
    out[...] = total.astype(BF)


def join_kernel(own, other, bit, out):
    half = own.shape[1]
    first = bit[0] == 0
    mine, came = own[...].astype(F32), other[...].astype(F32)
    left = jnp.where(first, mine, came).astype(BF)
    right = jnp.where(first, came, mine).astype(BF)
    for n in range(out.shape[0]):
        out[n, :, :half] = left
        out[n, :, half:] = right


def spread_kernel(scale, own, other, core, out):
    half = own.shape[0]
    first = core[0] == 0
    mine, came = own[...].astype(F32) * scale, other[...].astype(F32) * scale
    out[:half, :] = jnp.where(first, mine, came)
    out[half:, :] = jnp.where(first, came, mine)


def shift_sum(block, place, count, axis, perm):
    size = block.shape[0] // count

    def piece(at):
        return lax.dynamic_slice(
            block, (at * size, 0), (size, block.shape[1]), allow_negative_indices=False
        )

    came = [
        lax.ppermute(piece(lax.rem(place + k, count)), axis, perm(k)) for k in range(1, count)
    ]
    total = piece(place).astype(F32)
    for other in came:
        total = total + other.astype(F32)
    return total


def half_sum(block, bit, perm):
    size = block.shape[1] // 2

    def piece(at):
        return lax.dynamic_slice(
            block, (0, at * size), (block.shape[0], size), allow_negative_indices=False
        )

    came = lax.ppermute(piece(1 - bit), "dev", perm)
    return piece(bit) + came


def swap(block, step):
    return lax.ppermute(block, "dev", [(d, d ^ step) for d in range(lax.axis_size("dev"))])


def with_bit(kernel, out, own, other, bit):
    vmem = pl.BlockSpec(memory_space=pltpu.VMEM)
    return pl.pallas_call(
        kernel,
        out_shape=out,
        in_specs=[vmem, vmem, pl.BlockSpec(memory_space=pltpu.SMEM)],
        compiler_params=pltpu.CompilerParams(vmem_limit_bytes=16 * 1024 * 1024),
    )(own, other, bit.reshape(1))


def reduce_weight(partial, grp_count, dev_count):
    side = math.isqrt(grp_count)
    grp = lax.axis_index("grp")
    core = lax.axis_index("dev") & 1
    x, y = lax.div(grp, side), lax.rem(grp, side)

    def along_x(k):
        return [(g, (g // side + k) % side * side + g % side) for g in range(grp_count)]

    def along_y(k):
        return [(g, g // side * side + (g % side + k) % side) for g in range(grp_count)]

    def along_core(k):
        return [(d, d ^ k) for d in range(dev_count)]

    part = shift_sum(partial, core, 2, "dev", along_core).astype(BF)
    part = shift_sum(part, x, side, "grp", along_x).astype(BF)
    part = shift_sum(part, y, side, "grp", along_y)
    bit = (lax.axis_index("dev") >> 1) & 1
    part = half_sum(part, bit, along_core(2)).astype(BF)
    ring = [list(range(i, dev_count, 4)) for i in range(4)]
    every = lax.all_gather(part, "dev", axis_index_groups=ring, axis=0)
    shape = jax.ShapeDtypeStruct
    (own,) = call(ring_kernel, (shape(part.shape, BF),), (every,), 0)
    rows, half = part.shape
    return with_bit(
        join_kernel, shape((grp_count, rows, 2 * half), BF), own, swap(own, 2), bit
    )


def gather_weight(own, scale):
    grp_count, rows, lanes = own.shape
    own = own.reshape(grp_count * rows, lanes)
    out = jax.ShapeDtypeStruct((2 * grp_count * rows, lanes), F32)
    core = lax.axis_index("dev") & 1
    return with_bit(functools.partial(spread_kernel, scale), out, own, swap(own, 1), core)


def per_device(
    papers,
    authors,
    cotangent,
    w_self,
    w_cite,
    w_aut,
    bias,
    cite_col,
    edge_author,
    edge_dest,
    edge_row,
):
    dev_count = lax.axis_size("dev")
    grp_count = lax.axis_size("grp")
    pap_rows, width = papers.shape
    aut_rows = authors.shape[0]
    edges = edge_author.shape[0]
    slots = 2 * edges // dev_count
    total = dev_count * slots
    hidden = w_aut.shape[1]
    lines = dev_count * HALVES
    line = slots // HALVES * width + AUX
    shape = jax.ShapeDtypeStruct
    ends = jnp.stack([edge_dest[:, 0], edge_author, edge_row])

    (outgoing,) = call(
        functools.partial(pack_kernel, dev_count, slots),
        (shape((dev_count, HALVES, line), BF),),
        (authors, ends),
        2 * total * aut_rows * (edges + width),
    )
    arrived = lax.all_to_all(
        outgoing, "dev", 0, 0, tiled=True
    )
    forward = [(i, i + 1) for i in range(dev_count - 1)]
    backward = [(i + 1, i) for i in range(dev_count - 1)]
    low = lax.ppermute(papers[pap_rows - RIM :], "dev", forward)
    high = lax.ppermute(papers[:RIM], "dev", backward)
    base, owner = call(
        functools.partial(base_kernel, dev_count, slots),
        (shape((pap_rows, hidden), F32), shape((total, aut_rows), BF)),
        (papers, low, high, cite_col.T, w_self, w_cite, bias.reshape(1, hidden), ends),
        2 * pap_rows * width * (2 * hidden + pap_rows + 2 * RIM),
    )
    updated, slot_grad, side_rows, side_grad = call(
        node_kernel,
        (
            shape((pap_rows, hidden), BF),
            shape((total, hidden), BF),
            shape((total, width), BF),
            shape((total, hidden), BF),
        ),
        (arrived, base, cotangent, w_aut),
        2 * total * hidden * (width + 2 * pap_rows),
    )
    returned = lax.all_to_all(
        slot_grad.reshape(dev_count, slots, hidden), "dev", 0, 0, tiled=True
    ).reshape(total, hidden)
    (partial,) = call(
        weight_kernel,
        (shape((width, hidden), BF),),
        (side_rows, side_grad),
        2 * total * width * hidden,
    )
    copies = reduce_weight(partial, grp_count, dev_count)
    copies, returned = lax.optimization_barrier((copies, returned))
    own = lax.all_to_all(copies, "grp", 0, 0, tiled=True)
    (grad_authors,) = call(
        author_kernel,
        (shape((aut_rows, width), BF),),
        (returned, owner, w_aut),
        2 * aut_rows * hidden * (total + width),
    )
    own, grad_authors = lax.optimization_barrier((own, grad_authors))
    scale = 1.0 / math.sqrt(grp_count * dev_count * aut_rows)
    grad_w_aut = gather_weight(own, scale)
    return (updated, grad_authors, grad_w_aut)


def solution(mesh):
    placed = (
        P(("grp", "dev"), None),
        P(("grp", "dev"), None),
        P(("grp", "dev"), None),
        P(),
        P(),
        P(),
        P(),
        P(("grp", "dev"), None),
        P(("grp", "dev")),
        P(("grp", "dev"), None),
        P(("grp", "dev")),
    )
    return jax.shard_map(
        per_device,
        mesh=mesh,
        in_specs=placed,
        out_specs=(P(("grp", "dev"), None), P(("grp", "dev"), None), P()),
        check_vma=False,
    )
```
